32 devices in a mesh: parts: 2 (over y), blk: 4 (over x, core), rep: 4 (over z).
Axes of the slice: x: 2, y: 2, z: 4, core: 2. Of those that a mesh axis runs over, the one named last changes fastest.
Arguments:
- features: float32 [8192, 128], P(('parts', 'blk', 'rep')), parts along dimension 0, may hold values from -6 to 6
- neighbour_mean: float32 [8192, 128], P(('parts', 'blk', 'rep')), parts along dimension 0, may hold values from -6 to 6
- out_grad: float32 [8192, 256], P(('parts', 'blk', 'rep')), parts along dimension 0, may hold values from -6 to 6
- self_weight: float32 [128, 256], replicated, may hold values from -0.5 to 0.5
- neigh_weight: float32 [128, 256], replicated, may hold values from -0.5 to 0.5
- bias: float32 [256], replicated, may hold values from -4 to 4
- tile_values: float32 [8, 4, 4, 10, 128, 128], P(('parts', 'blk'), 'rep'), parts along dimension 0, may hold values from 0 to 0.03
- tile_coords: int32 [8, 4, 4, 10, 2], P(('parts', 'blk'), 'rep'), parts along dimension 0, may hold values from 0 to 7, as said below
- tile_counts: int32 [8, 4, 4], P(('parts', 'blk'), 'rep'), parts along dimension 0, may hold values from 1 to 10
Outputs:
- feature_grad: float32 [8192, 128], P(('parts', 'blk', 'rep')), parts along dimension 0
- self_grad: float32 [256, 256], P('parts'), parts along dimension 0
- neigh_grad: float32 [256, 256], P('parts'), parts along dimension 0
- bias_grad: float32 [512], P('parts'), parts along dimension 0
The draws below stay inside these ranges and needn't reach their ends.
There are 2 independent parts, one for each index of `parts`. The reference program is written for one: setup_inputs(seed, part) draws one part's arguments, and reference() takes and returns one part's arrays. A program takes and returns all parts, laid end to end along the dimension named above; an argument that names none is the same for every part. Nothing has to cross between parts.
Inputs may be any that keep to these rules, and one draw needn't show every extreme that they name: tile_coords[..., 0] is below 8 and tile_coords[..., 1] below 2; within one list of 10 slots the pairs are distinct.
All inputs are finite; a program needn't handle non-finite values.
Results may differ from the reference program's by a relative error of at most 0.0003.
Values sent between devices are 32-bit elements; how exact they have to be, the bound alone decides.
A program may use at most 64 MiB of HBM per device.

```python
import jax
import jax.numpy as jnp
from jax import lax

F = 128
H = 256
TILE = 128
TR = 2
TCAP = 10
BLOCKS = 4
REPS = 4
NODES = 4096


def draw_tile_coords(key, part):
    key = jax.random.fold_in(key, 2)
    pairs = REPS * TR * TR
    scores = jax.random.randint(key, (BLOCKS, REPS, BLOCKS, pairs), 0, 65536, dtype=jnp.int32)
    scores = scores * pairs + jnp.arange(pairs, dtype=jnp.int32)
    order = jnp.argsort(scores, axis=-1)[..., :TCAP].astype(jnp.int32)
    return jnp.stack([order // TR, order % TR], axis=-1).astype(jnp.int32)


def draw_tile_counts(key, part):
    key = jax.random.fold_in(key, 5)
    first_key, second_key = jax.random.split(key)
    base = jax.random.randint(first_key, (BLOCKS, REPS, BLOCKS), 1, TCAP + 1, dtype=jnp.int32)
    full_at = jax.random.randint(second_key, (BLOCKS, REPS), 0, BLOCKS, dtype=jnp.int32)
    column_ids = jnp.arange(BLOCKS, dtype=jnp.int32)
    return jnp.where(column_ids == full_at[..., None], TCAP, base).astype(jnp.int32)


def level_of(rng, dims, pieces, least, largest):
    level = 1.0
    for axis_at, blocks in pieces:
        draws = jax.random.uniform(jax.random.fold_in(jax.random.fold_in(rng, 6), axis_at), (blocks,), jnp.float32, least / len(pieces), largest / len(pieces))
        level = level * jnp.repeat(jnp.exp(draws), dims[axis_at] // blocks).reshape((-1,) + (1,) * (len(dims) - 1 - axis_at))
    return level


def noise(key, extent, deviation, reach, shards=(), kind=jnp.bfloat16):
    loudness = level_of(key, extent, shards, -0.22, 0.18) if shards else 1.0
    entries = jax.random.normal(key, extent, jnp.float32) * deviation * loudness
    return jnp.minimum(jnp.maximum(entries, -reach), reach).astype(kind)


def setup_inputs(seed: int = 0, part: int = 0) -> dict:
    key_list = jax.random.split(jax.random.key(seed), 10)
    part_keys = jax.random.split(jax.random.fold_in(key_list[9], part), 10)
    features = noise(part_keys[0], (NODES, F), 1.0, 6.0, ((0, 16),), jnp.float32)
    neighbour_mean = noise(part_keys[1], (NODES, F), 1.0, 6.0, ((0, 16),), jnp.float32)
    out_grad = noise(part_keys[2], (NODES, H), 1.0, 6.0, ((0, 16),), jnp.float32)
    self_weight = noise(key_list[3], (F, H), F ** -0.5, 0.5, (), jnp.float32)
    neigh_weight = noise(key_list[4], (F, H), F ** -0.5, 0.5, (), jnp.float32)
    bias = noise(key_list[5], (H,), 1.0, 4.0, (), jnp.float32)
    tile_values = jnp.clip(0.03 * jax.random.uniform(part_keys[6], (BLOCKS, REPS, BLOCKS, TCAP, TILE, TILE), jnp.float32) ** level_of(part_keys[6], (BLOCKS, REPS, BLOCKS, TCAP, TILE, TILE), ((0, 4), (1, 4)), -0.2, 0.2), 0.0, 0.03)
    tile_coords = draw_tile_coords(jax.random.fold_in(jax.random.fold_in(key_list[9], part), 71), part)
    tile_counts = draw_tile_counts(jax.random.fold_in(jax.random.fold_in(key_list[9], part), 71), part)
    return {"features": features, "neighbour_mean": neighbour_mean, "out_grad": out_grad, "self_weight": self_weight, "neigh_weight": neigh_weight, "bias": bias, "tile_values": tile_values, "tile_coords": tile_coords, "tile_counts": tile_counts}


def reference(features, neighbour_mean, out_grad, self_weight, neigh_weight, bias, tile_values, tile_coords, tile_counts):
    top_precision = lax.Precision.HIGHEST
    pre = jnp.dot(features, self_weight, precision=top_precision, preferred_element_type=jnp.float32)
    pre = pre + jnp.dot(neighbour_mean, neigh_weight, precision=top_precision, preferred_element_type=jnp.float32) + bias
    sigmoid_pre = jax.nn.sigmoid(pre)
    d_pre = out_grad * sigmoid_pre * (1.0 + pre * (1.0 - sigmoid_pre))
    d_agg = jnp.dot(d_pre, neigh_weight.T, precision=top_precision, preferred_element_type=jnp.float32)
    grad_blocks = d_agg.reshape(BLOCKS, REPS * TR, TILE, F)
    slot_ids = jnp.arange(TCAP, dtype=jnp.int32)
    column_ids = jnp.arange(TR, dtype=jnp.int32)

    def single_block(carry, inputs):
        rows_grad, tile_block, coords, tile_count = inputs
        chosen_tiles = rows_grad[coords[..., 0]]
        tile_products = jnp.einsum('rjtab,rjtaf->rjtbf', tile_block, chosen_tiles, precision=top_precision)
        live = slot_ids[:, None] < tile_count[..., None, None]
        select_tile = ((coords[..., 1][..., None] == column_ids) & live).astype(jnp.float32)
        contrib = jnp.einsum('rjtc,rjtbf->jrcbf', select_tile, tile_products, precision=top_precision)
        return carry + contrib, None

    start = jnp.zeros((BLOCKS, REPS, TR, TILE, F), jnp.float32)
    total, _ = lax.scan(single_block, start, (grad_blocks, tile_values, tile_coords, tile_counts))
    neighbour_grad = total.reshape(NODES, F)
    feature_grad = jnp.dot(d_pre, self_weight.T, precision=top_precision, preferred_element_type=jnp.float32) + neighbour_grad
    self_grad = jnp.dot(features.T, d_pre, precision=top_precision, preferred_element_type=jnp.float32)
    neigh_grad = jnp.dot(neighbour_mean.T, d_pre, precision=top_precision, preferred_element_type=jnp.float32)
    bias_grad = jnp.sum(d_pre, axis=0)
    return (feature_grad, self_grad, neigh_grad, bias_grad)
```

```python
import functools

import jax
import jax.numpy as jnp
from jax import lax
from jax.experimental import pallas as pl
from jax.experimental.pallas import tpu as pltpu
from jax.sharding import PartitionSpec as P

F = 128
H = 256
TILE = 128
TR = 2
TCAP = 10
MESH = pl.DeviceIdType.MESH
NN = (((1,), (0,)), ((), ()))
NT = (((1,), (1,)), ((), ()))


def split(x):
    hi = x.astype(jnp.bfloat16)
    return hi, (x - hi.astype(jnp.float32)).astype(jnp.bfloat16)


def dot3(a, b, dims):
    def one(p, q):
        return lax.dot_general(p, q, dims, preferred_element_type=jnp.float32)

    return one(a[0], b[0]) + (one(a[0], b[1]) + one(a[1], b[0]))


def kernel(
    blks, reps,
    feat, nm, og, ws, wn, bias, coords, counts, tiles,
    fg_out, sg_out, ng_out, bg_out,
    tv, th, tl, gather, gh, gl, lhs_h, lhs_l, dself,
    wbuf, wrecv, acc, tot_in, back, total,
    part, pair, sib_recv, far_recv,
    tile_sem, gs_sem, gr_sem, ws_sem, wr_sem, chain_s, chain_r, ts_sem, tr_sem,
    sib_s, sib_r, far_s, far_r,
):
    b = lax.axis_index("blk")
    z = lax.axis_index("rep")
    chips = blks // 2
    chip, core = b // 2, b % 2
    rows = 2 * F // blks
    has_left, has_right = z > 0, z < reps - 1

    def remote(src, dst, ssem, rsem, **where):
        return pltpu.make_async_remote_copy(
            src_ref=src, dst_ref=dst, send_sem=ssem, recv_sem=rsem,
            device_id=where, device_id_type=MESH,
        )

    barrier = pltpu.get_barrier_semaphore()
    for d in range(1, blks):
        pl.semaphore_signal(
            barrier, inc=1, device_id={"blk": (b + d) % blks}, device_id_type=MESH
        )

    @pl.when(has_left)
    def _():
        pl.semaphore_signal(barrier, inc=1, device_id={"rep": z - 1}, device_id_type=MESH)

    @pl.when(has_right)
    def _():
        pl.semaphore_signal(barrier, inc=1, device_id={"rep": z + 1}, device_id_type=MESH)

    tile_copies = [
        pltpu.make_async_copy(tiles.at[j], tv.at[j], tile_sem.at[j]) for j in range(blks)
    ]
    for c in tile_copies:
        c.start()

    x = jnp.concatenate([feat[...], nm[...]], axis=1)
    w = split(jnp.concatenate([ws[...], wn[...]], axis=0))
    pre = dot3(split(x), w, NN) + bias[...]
    sig = 1.0 / (1.0 + jnp.exp(-pre))
    d_pre = og[...] * sig * (1.0 + pre * (1.0 - sig))
    d_split = split(d_pre)
    dx = dot3(d_split, w, NT)
    for i in range(TR):
        gather[TR * z + i] = dx[i * TILE : (i + 1) * TILE, F:].T

    ends = jnp.where((z == 0) | (z == reps - 1), 1, 2)
    pl.semaphore_wait(barrier, blks - 1 + ends)

    def gather_copy(direction, step, i):
        block = z - step if direction == 0 else z + step
        to = z + 1 if direction == 0 else z - 1
        slot = gather.at[TR * block + i]
        return remote(
            slot, slot, gs_sem.at[direction, step, i], gr_sem.at[direction, step, i], rep=to
        )

    def sends(direction, step):
        if direction == 0:
            return (z >= step) & has_right
        return (z + step < reps) & has_left

    def receives(direction, step):
        if direction == 0:
            return z - 1 >= step
        return z + 1 + step < reps

    def split_block(slot):
        hi, lo = split(gather[slot])
        gh[slot] = hi
        gl[slot] = lo

    def gather_step(step):
        for i in range(TR):
            for direction in range(2):

                @pl.when(receives(direction, step))
                def _():
                    block = z - 1 - step if direction == 0 else z + 1 + step
                    slot = gather.at[TR * block + i]
                    remote(
                        slot, slot,
                        gs_sem.at[direction, step, i], gr_sem.at[direction, step, i],
                        rep=z - 1 if direction == 0 else z + 1,
                    ).wait_recv()
                    if step + 1 < reps - 1:

                        @pl.when(sends(direction, step + 1))
                        def _():
                            gather_copy(direction, step + 1, i).start()

        for i in range(TR):
            for direction in range(2):

                @pl.when(receives(direction, step))
                def _():
                    block = z - 1 - step if direction == 0 else z + 1 + step
                    split_block(TR * block + i)

    for i in range(TR):
        for direction in range(2):

            @pl.when(sends(direction, 0))
            def _():
                gather_copy(direction, 0, i).start()

    grad_w = dot3(split(x.T), d_split, NN)
    grad_b = jnp.broadcast_to(jnp.sum(d_pre, axis=0, keepdims=True), (8, H))
    for j in range(blks):
        wbuf[j, :rows] = grad_w[j * rows : (j + 1) * rows]
        wbuf[j, rows:] = grad_b
    w_copies = []
    for d in range(1, blks):
        to = (b + d) % blks
        w_copies.append(
            remote(wbuf.at[to], wrecv.at[d - 1], ws_sem.at[d - 1], wr_sem.at[d - 1], blk=to)
        )
    for c in w_copies:
        c.start()

    dself[...] = dx[:, :F]
    for i in range(TR):
        split_block(TR * z + i)

    def split_tiles(j):
        tile_copies[j].wait()
        hi, lo = split(tv[j])
        th[j] = hi
        tl[j] = lo

    gather_step(0)
    for j in range(blks // 2):
        split_tiles(j)

    for c in w_copies:
        c.wait_recv()
    own = wbuf[b]
    for d in range(1, blks):
        own = own + wrecv[d - 1]
    acc[...] = own
    left_half = z < reps // 2
    inner = jnp.where(left_half, z + 1, z - 1)
    outer = jnp.where(left_half, z - 1, z + 1)
    at_end = (z == 0) | (z == reps - 1)
    at_middle = (z == reps // 2 - 1) | (z == reps // 2)
    to_inner = remote(acc, tot_in, chain_s.at[0], chain_r.at[0], rep=inner)
    to_middle = remote(acc, back, chain_s.at[1], chain_r.at[1], rep=inner)
    to_outer = remote(total.at[b], back, chain_s.at[2], chain_r.at[1], rep=outer)

    @pl.when(jnp.logical_not(at_end))
    def _():
        remote(acc, tot_in, chain_s.at[0], chain_r.at[0], rep=outer).wait_recv()
        acc[...] = acc[...] + tot_in[...]

    @pl.when(jnp.logical_not(at_middle))
    def _():
        to_inner.start()

    @pl.when(at_middle)
    def _():
        to_middle.start()

    for step in range(1, reps - 1):
        gather_step(step)
        if step == 1:
            for j in range(blks // 2, blks):
                split_tiles(j)

    to_middle.wait_recv()

    @pl.when(at_middle)
    def _():
        total[b] = acc[...] + back[...]

    @pl.when(jnp.logical_not(at_middle))
    def _():
        total[b] = back[...]

    @pl.when(jnp.logical_not(at_end))
    def _():
        to_outer.start()

    t_copies = []
    for d in range(1, blks):
        t_copies.append(
            remote(total.at[b], total.at[b], ts_sem.at[d - 1], tr_sem.at[d - 1], blk=(b + d) % blks)
        )
    for c in t_copies:
        c.start()

    def product(j):
        for t in range(TCAP):
            row = coords[(j * TCAP + t) * 2]
            col = coords[(j * TCAP + t) * 2 + 1]
            live = (t < counts[j]).astype(jnp.int32)
            hi, lo = gh[row], gl[row]
            for c in range(TR):
                on = (live * (col == c).astype(jnp.int32)).astype(jnp.float32)
                mask = jnp.full((1, TILE), on, jnp.float32).astype(jnp.bfloat16)
                lhs_h[c * F : (c + 1) * F, t * TILE : (t + 1) * TILE] = hi * mask
                lhs_l[c * F : (c + 1) * F, t * TILE : (t + 1) * TILE] = lo * mask
        return dot3((lhs_h[...], lhs_l[...]), (th[j], tl[j]), NN)

    def to_sibling(d):
        return remote(
            part.at[d], sib_recv.at[d], sib_s.at[d], sib_r.at[d], blk=2 * chip + (1 - core)
        )

    def to_far(d):
        return remote(
            pair.at[d - 1], far_recv.at[d - 1], far_s.at[d - 1], far_r.at[d - 1],
            blk=2 * ((chip + d) % chips) + core,
        )

    for d in list(range(1, chips)) + [0]:
        at = (chip + d) % chips
        part[d] = product(2 * at + (1 - core))
        to_sibling(d).start()
        mine = product(2 * at + core)
        to_sibling(d).wait_recv()
        mine = mine + sib_recv[d]
        if d > 0:
            pair[d - 1] = mine
            to_far(d).start()

    for c in t_copies:
        c.wait_recv()
    half = blks // 2
    for j in range(half):
        sg_out[j * rows : (j + 1) * rows] = total[j, :rows]
        ng_out[j * rows : (j + 1) * rows] = total[half + j, :rows]
    bg_out[...] = total[0, rows : rows + 1]

    for d in range(1, chips):
        to_far(d).wait_recv()
        mine = mine + far_recv[d - 1]
    for i in range(TR):
        fg_out[i * TILE : (i + 1) * TILE] = (
            dself[i * TILE : (i + 1) * TILE] + mine[i * F : (i + 1) * F].T
        )

    for step in range(reps - 1):
        for i in range(TR):
            for direction in range(2):

                @pl.when(sends(direction, step))
                def _():
                    gather_copy(direction, step, i).wait_send()

    for c in w_copies + t_copies:
        c.wait_send()

    @pl.when(jnp.logical_not(at_middle))
    def _():
        to_inner.wait_send()

    @pl.when(at_middle)
    def _():
        to_middle.wait_send()

    @pl.when(jnp.logical_not(at_end))
    def _():
        to_outer.wait_send()

    for d in range(chips):
        to_sibling(d).wait_send()
    for d in range(1, chips):
        to_far(d).wait_send()


def on_device(blks, reps, features, neighbour_mean, out_grad, self_weight, neigh_weight, bias,
              tile_values, tile_coords, tile_counts):
    chips = blks // 2
    rows = 2 * F // blks
    nodes = TR * TILE
    f32, bf16 = jnp.float32, jnp.bfloat16
    vmem = pl.BlockSpec(memory_space=pltpu.VMEM)
    smem = pl.BlockSpec(memory_space=pltpu.SMEM)
    dma = pltpu.SemaphoreType.DMA
    chunk = (rows + 8, H)
    feature_grad, self_grad, neigh_grad, bias_grad = pl.pallas_call(
        functools.partial(kernel, blks, reps),
        out_shape=(
            jax.ShapeDtypeStruct((nodes, F), f32),
            jax.ShapeDtypeStruct((F, H), f32),
            jax.ShapeDtypeStruct((F, H), f32),
            jax.ShapeDtypeStruct((1, H), f32),
        ),
        in_specs=[vmem] * 6 + [smem, smem, pl.BlockSpec(memory_space=pl.ANY)],
        out_specs=(vmem,) * 4,
        scratch_shapes=[
            pltpu.VMEM((blks, TCAP * TILE, TILE), f32),
            pltpu.VMEM((blks, TCAP * TILE, TILE), bf16),
            pltpu.VMEM((blks, TCAP * TILE, TILE), bf16),
            pltpu.VMEM((reps * TR, F, TILE), f32),
            pltpu.VMEM((reps * TR, F, TILE), bf16),
            pltpu.VMEM((reps * TR, F, TILE), bf16),
            pltpu.VMEM((TR * F, TCAP * TILE), bf16),
            pltpu.VMEM((TR * F, TCAP * TILE), bf16),
            pltpu.VMEM((nodes, F), f32),
            pltpu.VMEM((blks,) + chunk, f32),
            pltpu.VMEM((blks - 1,) + chunk, f32),
            pltpu.VMEM(chunk, f32),
            pltpu.VMEM(chunk, f32),
            pltpu.VMEM(chunk, f32),
            pltpu.VMEM((blks,) + chunk, f32),
            pltpu.VMEM((chips, TR * F, TILE), f32),
            pltpu.VMEM((chips - 1, TR * F, TILE), f32),
            pltpu.VMEM((chips, TR * F, TILE), f32),
            pltpu.VMEM((chips - 1, TR * F, TILE), f32),
            dma((blks,)),
            dma((2, reps - 1, TR)), dma((2, reps - 1, TR)),
            dma((blks - 1,)), dma((blks - 1,)),
            dma((3,)), dma((2,)),
            dma((blks - 1,)), dma((blks - 1,)),
            dma((chips,)), dma((chips,)),
            dma((chips - 1,)), dma((chips - 1,)),
        ],
        compiler_params=pltpu.CompilerParams(
            collective_id=0, has_side_effects=True, vmem_limit_bytes=56 * 2**20
        ),
    )(
        features, neighbour_mean, out_grad, self_weight, neigh_weight, bias.reshape(1, H),
        tile_coords.reshape(-1), tile_counts.reshape(-1),
        tile_values.reshape(blks, TCAP * TILE, TILE),
    )
    return feature_grad, self_grad, neigh_grad, bias_grad.reshape(H)


def solution(mesh):
    return jax.shard_map(
        functools.partial(on_device, mesh.shape["blk"], mesh.shape["rep"]),
        mesh=mesh,
        in_specs=(
            P(("parts", "blk", "rep"), None),
            P(("parts", "blk", "rep"), None),
            P(("parts", "blk", "rep"), None),
            P(),
            P(),
            P(),
            P(("parts", "blk"), "rep", None, None, None, None),
            P(("parts", "blk"), "rep", None, None, None),
            P(("parts", "blk"), "rep", None),
        ),
        out_specs=(
            P(("parts", "blk", "rep"), None),
            P("parts", None),
            P("parts", None),
            P("parts"),
        ),
        check_vma=False,
    )
```

```python
import functools

import jax
import jax.numpy as jnp
from jax import lax
from jax.experimental import pallas as pl
from jax.experimental.pallas import tpu as pltpu
from jax.sharding import PartitionSpec as P

F = 128
H = 256
TILE = 128
TR = 2
TCAP = 10
MESH = pl.DeviceIdType.MESH
NN = (((1,), (0,)), ((), ()))
NT = (((1,), (1,)), ((), ()))


def split(x):
    hi = x.astype(jnp.bfloat16)
    return hi, (x - hi.astype(jnp.float32)).astype(jnp.bfloat16)


def dot3(a, b, dims):
    def one(p, q):
        return lax.dot_general(p, q, dims, preferred_element_type=jnp.float32)

    return one(a[0], b[0]) + (one(a[0], b[1]) + one(a[1], b[0]))


def kernel(
    blks, reps,
    feat, nm, og, ws, wn, bias, coords, counts, tiles,
    fg_out, sg_out, ng_out, bg_out,
    tv, th, tl, gather, gh, gl, lhs_h, lhs_l, dself,
    wbuf, wrecv, acc, tot_in, back, total,
    part, pair, sib_recv, far_recv,
    tile_sem, gs_sem, gr_sem, ws_sem, wr_sem, chain_s, chain_r, ts_sem, tr_sem,
    sib_s, sib_r, far_s, far_r,
):
    b = lax.axis_index("blk")
    z = lax.axis_index("rep")
    chips = blks // 2
    chip, core = b // 2, b % 2
    rows = 2 * F // blks
    has_left, has_right = z > 0, z < reps - 1

    def remote(src, dst, ssem, rsem, **where):
        return pltpu.make_async_remote_copy(
            src_ref=src, dst_ref=dst, send_sem=ssem, recv_sem=rsem,
            device_id=where, device_id_type=MESH,
        )

    barrier = pltpu.get_barrier_semaphore()
    for d in range(1, blks):
        pl.semaphore_signal(
            barrier, inc=1, device_id={"blk": (b + d) % blks}, device_id_type=MESH
        )

    @pl.when(has_left)
    def _():
        pl.semaphore_signal(barrier, inc=1, device_id={"rep": z - 1}, device_id_type=MESH)

    @pl.when(has_right)
    def _():
        pl.semaphore_signal(barrier, inc=1, device_id={"rep": z + 1}, device_id_type=MESH)

    tile_copies = [
        pltpu.make_async_copy(tiles.at[j], tv.at[j], tile_sem.at[j]) for j in range(blks)
    ]
    for c in tile_copies:
        c.start()

    x = jnp.concatenate([feat[...], nm[...]], axis=1)
    w = split(jnp.concatenate([ws[...], wn[...]], axis=0))
    pre = dot3(split(x), w, NN) + bias[...]
    sig = 1.0 / (1.0 + jnp.exp(-pre))
    d_pre = og[...] * sig * (1.0 + pre * (1.0 - sig))
    d_split = split(d_pre)
    dx = dot3(d_split, w, NT)
    for i in range(TR):
        gather[TR * z + i] = dx[i * TILE : (i + 1) * TILE, F:].T

    ends = jnp.where((z == 0) | (z == reps - 1), 1, 2)
    pl.semaphore_wait(barrier, blks - 1 + ends)

    def gather_copy(direction, step, i):
        block = z - step if direction == 0 else z + step
        to = z + 1 if direction == 0 else z - 1
        slot = gather.at[TR * block + i]
        return remote(
            slot, slot, gs_sem.at[direction, step, i], gr_sem.at[direction, step, i], rep=to
        )

    def sends(direction, step):
        if direction == 0:
            return (z >= step) & has_right
        return (z + step < reps) & has_left

    def receives(direction, step):
        if direction == 0:
            return z - 1 >= step
        return z + 1 + step < reps

    def split_block(slot):
        hi, lo = split(gather[slot])
        gh[slot] = hi
        gl[slot] = lo

    def gather_step(step):
        for i in range(TR):
            for direction in range(2):

                @pl.when(receives(direction, step))
                def _():
                    block = z - 1 - step if direction == 0 else z + 1 + step
                    slot = gather.at[TR * block + i]
                    remote(
                        slot, slot,
                        gs_sem.at[direction, step, i], gr_sem.at[direction, step, i],
                        rep=z - 1 if direction == 0 else z + 1,
                    ).wait_recv()
                    if step + 1 < reps - 1:

                        @pl.when(sends(direction, step + 1))
                        def _():
                            gather_copy(direction, step + 1, i).start()

        for i in range(TR):
            for direction in range(2):

                @pl.when(receives(direction, step))
                def _():
                    block = z - 1 - step if direction == 0 else z + 1 + step
                    split_block(TR * block + i)

    for i in range(TR):
        for direction in range(2):

            @pl.when(sends(direction, 0))
            def _():
                gather_copy(direction, 0, i).start()

    grad_w = dot3(split(x.T), d_split, NN)
    grad_b = jnp.broadcast_to(jnp.sum(d_pre, axis=0, keepdims=True), (8, H))
    for j in range(blks):
        wbuf[j, :rows] = grad_w[j * rows : (j + 1) * rows]
        wbuf[j, rows:] = grad_b
    w_copies = []
    for d in range(1, blks):
        to = (b + d) % blks
        w_copies.append(
            remote(wbuf.at[to], wrecv.at[d - 1], ws_sem.at[d - 1], wr_sem.at[d - 1], blk=to)
        )
    for c in w_copies:
        c.start()

    dself[...] = dx[:, :F]
    for i in range(TR):
        split_block(TR * z + i)

    def split_tiles(j):
        tile_copies[j].wait()
        hi, lo = split(tv[j])
        th[j] = hi
        tl[j] = lo

    gather_step(0)
    for j in range(blks // 2):
        split_tiles(j)

    for c in w_copies:
        c.wait_recv()
    own = wbuf[b]
    for d in range(1, blks):
        own = own + wrecv[d - 1]
    acc[...] = own
    left_half = z < reps // 2
    inner = jnp.where(left_half, z + 1, z - 1)
    outer = jnp.where(left_half, z - 1, z + 1)
    at_end = (z == 0) | (z == reps - 1)
    at_middle = (z == reps // 2 - 1) | (z == reps // 2)
    to_inner = remote(acc, tot_in, chain_s.at[0], chain_r.at[0], rep=inner)
    to_middle = remote(acc, back, chain_s.at[1], chain_r.at[1], rep=inner)
    to_outer = remote(total.at[b], back, chain_s.at[2], chain_r.at[1], rep=outer)

    @pl.when(at_end & jnp.logical_not(at_middle))
    def _():
        to_inner.start()

    for step in range(1, reps - 2):
        gather_step(step)

    @pl.when(jnp.logical_not(at_end))
    def _():
        remote(acc, tot_in, chain_s.at[0], chain_r.at[0], rep=outer).wait_recv()
        acc[...] = acc[...] + tot_in[...]

    @pl.when(jnp.logical_not(at_end | at_middle))
    def _():
        to_inner.start()

    @pl.when(at_middle)
    def _():
        to_middle.start()

    for j in range(blks // 2, blks):
        split_tiles(j)

    sibling = 2 * chip + (1 - core)

    def to_chip(d):
        mine = total.at[b]
        return remote(
            mine, mine, ts_sem.at[d - 1], tr_sem.at[d - 1], blk=2 * ((chip + d) % chips) + core
        )

    def pass_on(d):
        slot = total.at[2 * ((chip + chips - d) % chips) + core]
        at = chips - 1 + d
        return remote(slot, slot, ts_sem.at[at], tr_sem.at[at], blk=sibling)

    def spread():
        @pl.when(jnp.logical_not(at_end))
        def _():
            to_outer.start()

        for d in range(1, chips):
            to_chip(d).start()
        pass_on(0).start()

    @pl.when(at_middle)
    def _():
        to_middle.wait_recv()
        total[b] = acc[...] + back[...]
        spread()

    gather_step(reps - 2)

    def product(j):
        for t in range(TCAP):
            row = coords[j, 0, t]
            col = coords[j, 1, t]
            live = (t < counts[j]).astype(jnp.int32)
            hi, lo = gh[row], gl[row]
            for c in range(TR):
                on = (live * (col == c).astype(jnp.int32)).astype(jnp.float32)
                mask = jnp.full((1, TILE), on, jnp.float32).astype(jnp.bfloat16)
                lhs_h[c * F : (c + 1) * F, t * TILE : (t + 1) * TILE] = hi * mask
                lhs_l[c * F : (c + 1) * F, t * TILE : (t + 1) * TILE] = lo * mask
        return dot3((lhs_h[...], lhs_l[...]), (th[j], tl[j]), NN)

    def to_sibling(d):
        return remote(
            part.at[d], sib_recv.at[d], sib_s.at[d], sib_r.at[d], blk=sibling
        )

    def to_far(d):
        return remote(
            pair.at[d - 1], far_recv.at[d - 1], far_s.at[d - 1], far_r.at[d - 1],
            blk=2 * ((chip + d) % chips) + core,
        )

    def pair_sum(d):
        at = (chip + d) % chips
        part[d] = product(2 * at + (1 - core))
        to_sibling(d).start()
        mine = product(2 * at + core)
        to_sibling(d).wait_recv()
        return mine + sib_recv[d]

    for d in range(1, chips):
        pair[d - 1] = pair_sum(d)
        to_far(d).start()

    @pl.when(jnp.logical_not(at_middle))
    def _():
        to_middle.wait_recv()
        total[b] = back[...]
        spread()

    mine = pair_sum(0)

    for d in range(1, chips):
        to_chip(d).wait_recv()
        pass_on(d).start()
    for d in range(chips):
        pass_on(d).wait_recv()
    half = blks // 2
    for j in range(half):
        sg_out[j * rows : (j + 1) * rows] = total[j, :rows]
        ng_out[j * rows : (j + 1) * rows] = total[half + j, :rows]
    bg_out[...] = total[0, rows : rows + 1]

    for d in range(1, chips):
        to_far(d).wait_recv()
        mine = mine + far_recv[d - 1]
    for i in range(TR):
        fg_out[i * TILE : (i + 1) * TILE] = (
            dself[i * TILE : (i + 1) * TILE] + mine[i * F : (i + 1) * F].T
        )

    for step in range(reps - 1):
        for i in range(TR):
            for direction in range(2):

                @pl.when(sends(direction, step))
                def _():
                    gather_copy(direction, step, i).wait_send()

    for c in w_copies:
        c.wait_send()
    for d in range(1, chips):
        to_chip(d).wait_send()
    for d in range(chips):
        pass_on(d).wait_send()

    @pl.when(jnp.logical_not(at_middle))
    def _():
        to_inner.wait_send()

    @pl.when(at_middle)
    def _():
        to_middle.wait_send()

    @pl.when(jnp.logical_not(at_end))
    def _():
        to_outer.wait_send()

    for d in range(chips):
        to_sibling(d).wait_send()
    for d in range(1, chips):
        to_far(d).wait_send()


def hand_on(*refs):
    for source, target in zip(refs[:4], refs[4:]):
        target[...] = source[...]


def on_device(blks, reps, features, neighbour_mean, out_grad, self_weight, neigh_weight, bias,
              tile_values, tile_coords, tile_counts):
    chips = blks // 2
    rows = 2 * F // blks
    nodes = TR * TILE
    f32, bf16 = jnp.float32, jnp.bfloat16
    vmem = pl.BlockSpec(memory_space=pltpu.VMEM)
    smem = pl.BlockSpec(memory_space=pltpu.SMEM)
    dma = pltpu.SemaphoreType.DMA
    chunk = (rows + 8, H)
    feature_grad, self_grad, neigh_grad, bias_grad = pl.pallas_call(
        functools.partial(kernel, blks, reps),
        out_shape=(
            jax.ShapeDtypeStruct((nodes, F), f32),
            jax.ShapeDtypeStruct((F, H), f32),
            jax.ShapeDtypeStruct((F, H), f32),
            jax.ShapeDtypeStruct((1, H), f32),
        ),
        in_specs=[vmem] * 6 + [smem, smem, pl.BlockSpec(memory_space=pl.ANY)],
        out_specs=(vmem,) * 4,
        scratch_shapes=[
            pltpu.VMEM((blks, TCAP * TILE, TILE), f32),
            pltpu.VMEM((blks, TCAP * TILE, TILE), bf16),
            pltpu.VMEM((blks, TCAP * TILE, TILE), bf16),
            pltpu.VMEM((reps * TR, F, TILE), f32),
            pltpu.VMEM((reps * TR, F, TILE), bf16),
            pltpu.VMEM((reps * TR, F, TILE), bf16),
            pltpu.VMEM((TR * F, TCAP * TILE), bf16),
            pltpu.VMEM((TR * F, TCAP * TILE), bf16),
            pltpu.VMEM((nodes, F), f32),
            pltpu.VMEM((blks,) + chunk, f32),
            pltpu.VMEM((blks - 1,) + chunk, f32),
            pltpu.VMEM(chunk, f32),
            pltpu.VMEM(chunk, f32),
            pltpu.VMEM(chunk, f32),
            pltpu.VMEM((blks,) + chunk, f32),
            pltpu.VMEM((chips, TR * F, TILE), f32),
            pltpu.VMEM((chips - 1, TR * F, TILE), f32),
            pltpu.VMEM((chips, TR * F, TILE), f32),
            pltpu.VMEM((chips - 1, TR * F, TILE), f32),
            dma((blks,)),
            dma((2, reps - 1, TR)), dma((2, reps - 1, TR)),
            dma((blks - 1,)), dma((blks - 1,)),
            dma((3,)), dma((2,)),
            dma((blks - 1,)), dma((blks - 1,)),
            dma((chips,)), dma((chips,)),
            dma((chips - 1,)), dma((chips - 1,)),
        ],
        compiler_params=pltpu.CompilerParams(
            collective_id=0, has_side_effects=True, vmem_limit_bytes=56 * 2**20
        ),
    )(
        features, neighbour_mean, out_grad, self_weight, neigh_weight, bias.reshape(1, H),
        jnp.swapaxes(tile_coords, 3, 4).reshape(blks, 2, TCAP), tile_counts.reshape(-1),
        tile_values.reshape(blks, TCAP * TILE, TILE),
    )
    results = (feature_grad, self_grad, neigh_grad, bias_grad)
    feature_grad, self_grad, neigh_grad, bias_grad = pl.pallas_call(
        hand_on,
        out_shape=tuple(jax.ShapeDtypeStruct(a.shape, a.dtype) for a in results),
        in_specs=[vmem] * 4,
        out_specs=(vmem,) * 4,
    )(*results)
    return feature_grad, self_grad, neigh_grad, bias_grad.reshape(H)


def solution(mesh):
    return jax.shard_map(
        functools.partial(on_device, mesh.shape["blk"], mesh.shape["rep"]),
        mesh=mesh,
        in_specs=(
            P(("parts", "blk", "rep"), None),
            P(("parts", "blk", "rep"), None),
            P(("parts", "blk", "rep"), None),
            P(),
            P(),
            P(),
            P(("parts", "blk"), "rep", None, None, None, None),
            P(("parts", "blk"), "rep", None, None, None),
            P(("parts", "blk"), "rep", None),
        ),
        out_specs=(
            P(("parts", "blk", "rep"), None),
            P("parts", None),
            P("parts", None),
            P("parts"),
        ),
        check_vma=False,
    )
```

```python
import functools

import jax
import jax.numpy as jnp
from jax import lax
from jax.experimental import pallas as pl
from jax.experimental.pallas import tpu as pltpu
from jax.sharding import PartitionSpec as P

F = 128
H = 256
TILE = 128
TR = 2
TCAP = 10
MESH = pl.DeviceIdType.MESH
NN = (((1,), (0,)), ((), ()))
NT = (((1,), (1,)), ((), ()))


def split(x):
    hi = x.astype(jnp.bfloat16)
    return hi, (x - hi.astype(jnp.float32)).astype(jnp.bfloat16)


def dot3(a, b, dims):
    def one(p, q):
        return lax.dot_general(p, q, dims, preferred_element_type=jnp.float32)

    return one(a[0], b[0]) + (one(a[0], b[1]) + one(a[1], b[0]))


def kernel(
    blks, reps,
    feat, nm, og, ws, wn, bias, coords, counts, tiles,
    fg_out, sg_out, ng_out, bg_out,
    tv, th, tl, gather, gh, gl, lhs_h, lhs_l, dself,
    wbuf, wrecv, acc, tot_in, back, total,
    part, pair, sib_recv, far_recv,
    tile_sem, gs_sem, gr_sem, ws_sem, wr_sem, chain_s, chain_r, ts_sem, tr_sem,
    sib_s, sib_r, far_s, far_r,
):
    b = lax.axis_index("blk")
    z = lax.axis_index("rep")
    chips = blks // 2
    chip, core = b // 2, b % 2
    rows = 2 * F // blks
    has_left, has_right = z > 0, z < reps - 1

    def remote(src, dst, ssem, rsem, **where):
        return pltpu.make_async_remote_copy(
            src_ref=src, dst_ref=dst, send_sem=ssem, recv_sem=rsem,
            device_id=where, device_id_type=MESH,
        )

    barrier = pltpu.get_barrier_semaphore()
    for d in range(1, blks):
        pl.semaphore_signal(
            barrier, inc=1, device_id={"blk": (b + d) % blks}, device_id_type=MESH
        )

    @pl.when(has_left)
    def _():
        pl.semaphore_signal(barrier, inc=1, device_id={"rep": z - 1}, device_id_type=MESH)

    @pl.when(has_right)
    def _():
        pl.semaphore_signal(barrier, inc=1, device_id={"rep": z + 1}, device_id_type=MESH)

    tile_copies = [
        pltpu.make_async_copy(tiles.at[j], tv.at[j], tile_sem.at[j]) for j in range(blks)
    ]
    for c in tile_copies:
        c.start()

    x = jnp.concatenate([feat[...], nm[...]], axis=1)
    w = split(jnp.concatenate([ws[...], wn[...]], axis=0))
    pre = dot3(split(x), w, NN) + bias[...]
    sig = 1.0 / (1.0 + jnp.exp(-pre))
    d_pre = og[...] * sig * (1.0 + pre * (1.0 - sig))
    d_split = split(d_pre)
    dx = dot3(d_split, w, NT)
    for i in range(TR):
        gather[TR * z + i] = dx[i * TILE : (i + 1) * TILE, F:].T

    ends = jnp.where((z == 0) | (z == reps - 1), 1, 2)
    pl.semaphore_wait(barrier, blks - 1 + ends)

    def gather_copy(direction, step, i):
        block = z - step if direction == 0 else z + step
        to = z + 1 if direction == 0 else z - 1
        slot = gather.at[TR * block + i]
        return remote(
            slot, slot, gs_sem.at[direction, step, i], gr_sem.at[direction, step, i], rep=to
        )

    def sends(direction, step):
        if direction == 0:
            return (z >= step) & has_right
        return (z + step < reps) & has_left

    def receives(direction, step):
        if direction == 0:
            return z - 1 >= step
        return z + 1 + step < reps

    def split_block(slot):
        hi, lo = split(gather[slot])
        gh[slot] = hi
        gl[slot] = lo

    def gather_step(step):
        for i in range(TR):
            for direction in range(2):

                @pl.when(receives(direction, step))
                def _():
                    block = z - 1 - step if direction == 0 else z + 1 + step
                    slot = gather.at[TR * block + i]
                    remote(
                        slot, slot,
                        gs_sem.at[direction, step, i], gr_sem.at[direction, step, i],
                        rep=z - 1 if direction == 0 else z + 1,
                    ).wait_recv()
                    if step + 1 < reps - 1:

                        @pl.when(sends(direction, step + 1))
                        def _():
                            gather_copy(direction, step + 1, i).start()

        for i in range(TR):
            for direction in range(2):

                @pl.when(receives(direction, step))
                def _():
                    block = z - 1 - step if direction == 0 else z + 1 + step
                    split_block(TR * block + i)

    for i in range(TR):
        for direction in range(2):

            @pl.when(sends(direction, 0))
            def _():
                gather_copy(direction, 0, i).start()

    grad_w = dot3(split(x.T), d_split, NN)
    grad_b = jnp.broadcast_to(jnp.sum(d_pre, axis=0, keepdims=True), (8, H))
    for j in range(blks):
        wbuf[j, :rows] = grad_w[j * rows : (j + 1) * rows]
        wbuf[j, rows:] = grad_b
    w_copies = []
    for d in range(1, blks):
        to = (b + d) % blks
        w_copies.append(
            remote(wbuf.at[to], wrecv.at[d - 1], ws_sem.at[d - 1], wr_sem.at[d - 1], blk=to)
        )
    for c in w_copies:
        c.start()

    dself[...] = dx[:, :F]
    for i in range(TR):
        split_block(TR * z + i)

    def split_tiles(j):
        tile_copies[j].wait()
        hi, lo = split(tv[j])
        th[j] = hi
        tl[j] = lo

    gather_step(0)
    for j in range(blks // 2):
        split_tiles(j)

    for c in w_copies:
        c.wait_recv()
    own = wbuf[b]
    for d in range(1, blks):
        own = own + wrecv[d - 1]
    acc[...] = own
    left_half = z < reps // 2
    inner = jnp.where(left_half, z + 1, z - 1)
    outer = jnp.where(left_half, z - 1, z + 1)
    at_end = (z == 0) | (z == reps - 1)
    at_middle = (z == reps // 2 - 1) | (z == reps // 2)
    first = (rows + 8) // 16 * 8
    pieces = [pl.ds(0, first), pl.ds(first, rows + 8 - first)]

    def to_inner(h):
        return remote(
            acc.at[pieces[h]], tot_in.at[pieces[h]], chain_s.at[0, h], chain_r.at[0, h], rep=inner
        )

    def from_outer(h):
        return remote(
            acc.at[pieces[h]], tot_in.at[pieces[h]], chain_s.at[0, h], chain_r.at[0, h], rep=outer
        )

    def to_middle(h):
        return remote(
            acc.at[pieces[h]], back.at[pieces[h]], chain_s.at[1, h], chain_r.at[1, h], rep=inner
        )

    def to_outer(h):
        return remote(
            total.at[b, pieces[h]], back.at[pieces[h]], chain_s.at[2, h], chain_r.at[1, h], rep=outer
        )

    @pl.when(at_end & jnp.logical_not(at_middle))
    def _():
        for h in range(2):
            to_inner(h).start()

    for step in range(1, reps - 2):
        gather_step(step)

    for j in range(blks // 2, blks):
        split_tiles(j)

    for h in range(2):

        @pl.when(jnp.logical_not(at_end))
        def _():
            from_outer(h).wait_recv()
            acc[pieces[h]] = acc[pieces[h]] + tot_in[pieces[h]]

        @pl.when(jnp.logical_not(at_end | at_middle))
        def _():
            to_inner(h).start()

        @pl.when(at_middle)
        def _():
            to_middle(h).start()

    sibling = 2 * chip + (1 - core)

    def to_chip(d, h):
        mine = total.at[b, pieces[h]]
        return remote(
            mine, mine, ts_sem.at[d - 1, h], tr_sem.at[d - 1, h],
            blk=2 * ((chip + d) % chips) + core,
        )

    def pass_on(d, h):
        slot = total.at[2 * ((chip + chips - d) % chips) + core, pieces[h]]
        at = chips - 1 + d
        return remote(slot, slot, ts_sem.at[at, h], tr_sem.at[at, h], blk=sibling)

    gather_step(reps - 2)

    def product(j):
        for t in range(TCAP):
            row = coords[j, 0, t]
            col = coords[j, 1, t]
            live = (t < counts[j]).astype(jnp.int32)
            hi, lo = gh[row], gl[row]
            for c in range(TR):
                on = (live * (col == c).astype(jnp.int32)).astype(jnp.float32)
                mask = jnp.full((1, TILE), on, jnp.float32).astype(jnp.bfloat16)
                lhs_h[c * F : (c + 1) * F, t * TILE : (t + 1) * TILE] = hi * mask
                lhs_l[c * F : (c + 1) * F, t * TILE : (t + 1) * TILE] = lo * mask
        return dot3((lhs_h[...], lhs_l[...]), (th[j], tl[j]), NN)

    def to_sibling(d):
        return remote(
            part.at[d], sib_recv.at[d], sib_s.at[d], sib_r.at[d], blk=sibling
        )

    def to_far(d):
        return remote(
            pair.at[d - 1], far_recv.at[d - 1], far_s.at[d - 1], far_r.at[d - 1],
            blk=2 * ((chip + d) % chips) + core,
        )

    def pair_sum(d):
        at = (chip + d) % chips
        part[d] = product(2 * at + (1 - core))
        to_sibling(d).start()
        mine = product(2 * at + core)
        to_sibling(d).wait_recv()
        return mine + sib_recv[d]

    for d in range(1, chips):
        pair[d - 1] = pair_sum(d)
        to_far(d).start()

    for h in range(2):
        to_middle(h).wait_recv()

        @pl.when(at_middle)
        def _():
            total[b, pieces[h]] = acc[pieces[h]] + back[pieces[h]]

        @pl.when(jnp.logical_not(at_middle))
        def _():
            total[b, pieces[h]] = back[pieces[h]]

        @pl.when(jnp.logical_not(at_end))
        def _():
            to_outer(h).start()

        for d in range(1, chips):
            to_chip(d, h).start()
        pass_on(0, h).start()

    mine = pair_sum(0)

    for d in range(1, chips):
        for h in range(2):
            to_chip(d, h).wait_recv()
            pass_on(d, h).start()
    for d in range(chips):
        for h in range(2):
            pass_on(d, h).wait_recv()
    half = blks // 2
    for j in range(half):
        sg_out[j * rows : (j + 1) * rows] = total[j, :rows]
        ng_out[j * rows : (j + 1) * rows] = total[half + j, :rows]
    bg_out[...] = total[0, rows : rows + 1]

    for d in range(1, chips):
        to_far(d).wait_recv()
        mine = mine + far_recv[d - 1]
    for i in range(TR):
        fg_out[i * TILE : (i + 1) * TILE] = (
            dself[i * TILE : (i + 1) * TILE] + mine[i * F : (i + 1) * F].T
        )

    for step in range(reps - 1):
        for i in range(TR):
            for direction in range(2):

                @pl.when(sends(direction, step))
                def _():
                    gather_copy(direction, step, i).wait_send()

    for c in w_copies:
        c.wait_send()
    for h in range(2):
        for d in range(1, chips):
            to_chip(d, h).wait_send()
        for d in range(chips):
            pass_on(d, h).wait_send()

        @pl.when(jnp.logical_not(at_middle))
        def _():
            to_inner(h).wait_send()

        @pl.when(at_middle)
        def _():
            to_middle(h).wait_send()

        @pl.when(jnp.logical_not(at_end))
        def _():
            to_outer(h).wait_send()

    for d in range(chips):
        to_sibling(d).wait_send()
    for d in range(1, chips):
        to_far(d).wait_send()


def hand_on(*refs):
    for source, target in zip(refs[:4], refs[4:]):
        target[...] = source[...]


def on_device(blks, reps, features, neighbour_mean, out_grad, self_weight, neigh_weight, bias,
              tile_values, tile_coords, tile_counts):
    chips = blks // 2
    rows = 2 * F // blks
    nodes = TR * TILE
    f32, bf16 = jnp.float32, jnp.bfloat16
    vmem = pl.BlockSpec(memory_space=pltpu.VMEM)
    smem = pl.BlockSpec(memory_space=pltpu.SMEM)
    dma = pltpu.SemaphoreType.DMA
    chunk = (rows + 8, H)
    feature_grad, self_grad, neigh_grad, bias_grad = pl.pallas_call(
        functools.partial(kernel, blks, reps),
        out_shape=(
            jax.ShapeDtypeStruct((nodes, F), f32),
            jax.ShapeDtypeStruct((F, H), f32),
            jax.ShapeDtypeStruct((F, H), f32),
            jax.ShapeDtypeStruct((1, H), f32),
        ),
        in_specs=[vmem] * 6 + [smem, smem, pl.BlockSpec(memory_space=pl.ANY)],
        out_specs=(vmem,) * 4,
        scratch_shapes=[
            pltpu.VMEM((blks, TCAP * TILE, TILE), f32),
            pltpu.VMEM((blks, TCAP * TILE, TILE), bf16),
            pltpu.VMEM((blks, TCAP * TILE, TILE), bf16),
            pltpu.VMEM((reps * TR, F, TILE), f32),
            pltpu.VMEM((reps * TR, F, TILE), bf16),
            pltpu.VMEM((reps * TR, F, TILE), bf16),
            pltpu.VMEM((TR * F, TCAP * TILE), bf16),
            pltpu.VMEM((TR * F, TCAP * TILE), bf16),
            pltpu.VMEM((nodes, F), f32),
            pltpu.VMEM((blks,) + chunk, f32),
            pltpu.VMEM((blks - 1,) + chunk, f32),
            pltpu.VMEM(chunk, f32),
            pltpu.VMEM(chunk, f32),
            pltpu.VMEM(chunk, f32),
            pltpu.VMEM((blks,) + chunk, f32),
            pltpu.VMEM((chips, TR * F, TILE), f32),
            pltpu.VMEM((chips - 1, TR * F, TILE), f32),
            pltpu.VMEM((chips, TR * F, TILE), f32),
            pltpu.VMEM((chips - 1, TR * F, TILE), f32),
            dma((blks,)),
            dma((2, reps - 1, TR)), dma((2, reps - 1, TR)),
            dma((blks - 1,)), dma((blks - 1,)),
            dma((3, 2)), dma((2, 2)),
            dma((blks - 1, 2)), dma((blks - 1, 2)),
            dma((chips,)), dma((chips,)),
            dma((chips - 1,)), dma((chips - 1,)),
        ],
        compiler_params=pltpu.CompilerParams(
            collective_id=0, has_side_effects=True, vmem_limit_bytes=56 * 2**20
        ),
    )(
        features, neighbour_mean, out_grad, self_weight, neigh_weight, bias.reshape(1, H),
        jnp.swapaxes(tile_coords, 3, 4).reshape(blks, 2, TCAP), tile_counts.reshape(-1),
        tile_values.reshape(blks, TCAP * TILE, TILE),
    )
    results = (feature_grad, self_grad, neigh_grad, bias_grad)
    feature_grad, self_grad, neigh_grad, bias_grad = pl.pallas_call(
        hand_on,
        out_shape=tuple(jax.ShapeDtypeStruct(a.shape, a.dtype) for a in results),
        in_specs=[vmem] * 4,
        out_specs=(vmem,) * 4,
    )(*results)
    return feature_grad, self_grad, neigh_grad, bias_grad.reshape(H)


def solution(mesh):
    return jax.shard_map(
        functools.partial(on_device, mesh.shape["blk"], mesh.shape["rep"]),
        mesh=mesh,
        in_specs=(
            P(("parts", "blk", "rep"), None),
            P(("parts", "blk", "rep"), None),
            P(("parts", "blk", "rep"), None),
            P(),
            P(),
            P(),
            P(("parts", "blk"), "rep", None, None, None, None),
            P(("parts", "blk"), "rep", None, None, None),
            P(("parts", "blk"), "rep", None),
        ),
        out_specs=(
            P(("parts", "blk", "rep"), None),
            P("parts", None),
            P("parts", None),
            P("parts"),
        ),
        check_vma=False,
    )
```
